1024 devices in a mesh: expert: 64 (over z, x), tensor: 16 (over y, core).
Axes of the slice: x: 4, y: 8, z: 16, core: 2. Of those that a mesh axis runs over, the one named last changes fastest.
Arguments:
- tokens: bfloat16 [4096, 1536], P('expert'), may hold values from -6 to 6
- exponents: int32 [4096, 12], P('expert'), may hold values from -1 to 1
- out_grad: bfloat16 [4096, 1536], P('expert'), may hold values from -6 to 6
- slots: int32 [64, 128], replicated, may hold values from 0 to 4095, as said below
- gates: float32 [64, 128], P('expert'), may hold values from 0.1 to 1
- w_in: bfloat16 [64, 1536, 4096], P('expert', None, 'tensor'), may hold values from -0.15625 to 0.15625
- w_out: bfloat16 [64, 4096, 1536], P('expert', 'tensor'), may hold values from -0.09375 to 0.09375
Outputs:
- token_grad: bfloat16 [4096, 1536], P(('expert', 'tensor'))
- w_in_grad: bfloat16 [64, 1536, 4096], P('expert', None, 'tensor')
- w_out_grad: bfloat16 [64, 4096, 1536], P('expert', 'tensor')
- gate_grad: float32 [64, 128], P('expert')
The draws below stay inside these ranges and needn't reach their ends.
Inputs may be any that keep to these rules, and one draw needn't show every extreme that they name: `slots`: each row holds 128 distinct token indices. In every row, at most 2 indices fall in any aligned block of 64 tokens (the tokens of one index of expert), and some block holds exactly 2.
All inputs are finite; a program needn't handle non-finite values.
Results may differ from the reference program's by a relative error of at most 0.007.
Values may be sent and summed in bfloat16 or wider, within the bound.
No kernel may reach another device: no remote copies, remote signals or barrier semaphores. Data moves between devices by JAX's collectives and lax.ppermute only.
A program may use at most 32 MiB of HBM per device.

```python
import jax
import jax.numpy as jnp
from jax import lax

D = 1536
H = 4096
TOK_DEV = 64
E = 64
TOKENS = 4096
C = 128
BLOCKS = 12


def row_perms(key, row_count, length):
    return jax.vmap(lambda sub_key: jax.random.permutation(sub_key, length))(jax.random.split(key, row_count))


def draw_slots(key, part):
    key = jax.random.fold_in(key, 11)
    key_shard, key_popular, key_jitter, key_order = jax.random.split(key, 4)
    average = C // E
    spread = C // (4 * E)
    shard_perm = row_perms(key_shard, E, E)
    shard_rank = jnp.argsort(shard_perm, axis=1)
    counts = jnp.where(shard_rank < E // 2, average + spread, average - spread)
    popular = jax.random.randint(key_popular, (TOKENS,), 0, 4)
    jitter = jax.random.randint(key_jitter, (E, TOKENS), 0, 8)
    within = jnp.arange(TOKENS) % TOK_DEV
    scores = (popular[None, :] * 8 + jitter) * TOK_DEV + within[None, :]
    scores = scores.reshape(E, E, TOK_DEV)
    ranking = jnp.argsort(-scores, axis=2)
    position = jnp.argsort(ranking, axis=2)
    picked = (position < counts[:, :, None]).reshape(E, TOKENS)
    chosen = jnp.argsort(jnp.where(picked, 0, 1), axis=1, stable=True)[:, :C]
    shuffle = row_perms(key_order, E, C)
    return jnp.take_along_axis(chosen, shuffle, axis=1).astype(jnp.int32)


def with_ends(array, own_key, smallest, top_value):
    longest = array.shape.index(max(array.shape))
    spots = []
    for shift in (0, 1):
        where = [jax.random.randint(jax.random.fold_in(own_key, axis), (), 0, length) for axis, length in enumerate(array.shape)]
        where[longest] = (where[longest] + shift) % array.shape[longest]
        spots.append(tuple(where))
    return array.at[spots[0]].set(smallest).at[spots[1]].set(top_value)


def steps_of(stream_key, dims, cuts, smallest, largest):
    def one(dim, blocks):
        heights = jax.random.uniform(jax.random.fold_in(jax.random.fold_in(stream_key, 6), dim), (blocks,), jnp.float32, smallest / len(cuts), largest / len(cuts))
        return jnp.repeat(jnp.exp(heights), dims[dim] // blocks).reshape((-1,) + (1,) * (len(dims) - dim - 1))

    gain = one(*cuts[0])
    for cut in cuts[1:]:
        gain = gain * one(*cut)
    return gain


def scatter_about(stream_key, shape, scale, limit, pieces=(), kind=jnp.bfloat16):
    gain = steps_of(stream_key, shape, pieces, -0.22, 0.18) if pieces else 1.0
    values = jax.random.normal(stream_key, shape, jnp.float32) * scale * gain
    return jnp.minimum(jnp.maximum(values, -limit), limit).astype(kind)


def setup_inputs(seed: int = 0) -> dict:
    arg_keys = jax.random.split(jax.random.key(seed), 8)
    tokens = scatter_about(arg_keys[0], (TOKENS, D), 1.0, 6.0, ((0, 64),))
    exponents = with_ends(jax.random.randint(arg_keys[1], (TOKENS, BLOCKS), -1, 2), jax.random.fold_in(arg_keys[1], 1), -1, 1).astype(jnp.int32)
    out_grad = scatter_about(arg_keys[2], (TOKENS, D), 1.0, 6.0, ((0, 64),))
    slots = draw_slots(jax.random.fold_in(arg_keys[7], 71), 0)
    gates = jnp.clip(0.1 + 0.9 * jax.random.uniform(arg_keys[4], (E, C), jnp.float32) ** steps_of(arg_keys[4], (E, C), ((0, 64),), -0.2, 0.2), 0.1, 1.0)
    w_in = scatter_about(arg_keys[5], (E, D, H), D ** -0.5, 0.15625, ((0, 64), (2, 16)))
    w_out = scatter_about(arg_keys[6], (E, H, D), H ** -0.5, 0.09375, ((0, 64), (1, 16)))
    return {"tokens": tokens, "exponents": exponents, "out_grad": out_grad, "slots": slots, "gates": gates, "w_in": w_in, "w_out": w_out}


def contract(left, right, left_dim, right_dim):
    return lax.dot_general(left, right, (((left_dim,), (right_dim,)), ((), ())), preferred_element_type=jnp.float32)

def apply_scales(values, exponents):
    row_count = values.shape[0]
    factors = jnp.exp2(exponents.astype(jnp.float32))
    widened = values.astype(jnp.float32).reshape(row_count, BLOCKS, 128) * factors[:, :, None]
    return widened.reshape(row_count, D)

def reference(tokens, exponents, out_grad, slots, gates, w_in, w_out):
    scaled = apply_scales(tokens, exponents).astype(jnp.bfloat16)

    def one_expert(accumulated, item):
        picked_rows, gate_row, weight_in, weight_out = item
        slot_rows = scaled[picked_rows]
        slot_grads = out_grad[picked_rows]
        preact = jnp.dot(slot_rows, weight_in, preferred_element_type=jnp.float32)
        hidden_full, backward = jax.vjp(jax.nn.gelu, preact)
        hidden = hidden_full.astype(jnp.bfloat16)
        upstream = contract(slot_grads, weight_out, 1, 1)
        gate_part = lax.optimization_barrier(jnp.sum(hidden.astype(jnp.float32) * upstream, axis=1))
        dpre = backward(gate_row[:, None] * upstream)[0].astype(jnp.bfloat16)
        gated_grads = (gate_row[:, None] * slot_grads.astype(jnp.float32)).astype(jnp.bfloat16)
        out_weight_grad = contract(hidden, gated_grads, 0, 0).astype(jnp.bfloat16)
        in_weight_grad = contract(slot_rows, dpre, 0, 0).astype(jnp.bfloat16)
        slot_back = contract(dpre, weight_in, 1, 1)
        accumulated = accumulated.at[picked_rows].add(slot_back)
        return (accumulated, (in_weight_grad, out_weight_grad, gate_part))
    start = jnp.zeros((TOKENS, D), jnp.float32)
    summed, (w_in_grad, w_out_grad, gate_grad) = lax.scan(one_expert, start, (slots, gates, w_in, w_out))
    token_grad = apply_scales(summed, exponents).astype(jnp.bfloat16)
    return (token_grad, w_in_grad, w_out_grad, gate_grad)
```

```python
import jax
import jax.numpy as jnp
from jax import lax
from jax.sharding import PartitionSpec as P


def contract(left, right, left_dim, right_dim):
    return lax.dot_general(
        left, right, (((left_dim,), (right_dim,)), ((), ())), preferred_element_type=jnp.float32
    )


def apply_scales(values, exponents):
    row_count = values.shape[0]
    block_count = exponents.shape[1]
    factors = jnp.exp2(exponents.astype(jnp.float32))
    widened = values.astype(jnp.float32).reshape(row_count, block_count, 128) * factors[:, :, None]
    return widened.reshape(row_count, block_count * 128)


def local(tokens, exponents, out_grad, slots, gates, w_in, w_out):
    expert_count = lax.axis_size("expert")
    tensor_count = lax.axis_size("tensor")
    my_expert = lax.axis_index("expert")
    my_tensor = lax.axis_index("tensor")
    core = my_tensor % 2
    swap = [(index, index ^ 1) for index in range(tensor_count)]
    tok_count, width = tokens.shape
    half = width // 2
    half_blocks = exponents.shape[1] // 2
    slot_count = slots.shape[1]

    local_index = slots % tok_count
    from_here = slots // tok_count == my_expert
    lower = jnp.min(jnp.where(from_here, local_index, tok_count), axis=1)
    upper = jnp.max(jnp.where(from_here, local_index, -1), axis=1)
    picked = jnp.stack([lower, upper], axis=1).reshape(slot_count)
    pick = (picked[:, None] == jnp.arange(tok_count)[None, :]).astype(jnp.bfloat16)

    scaled = apply_scales(
        lax.dynamic_slice_in_dim(tokens, core * half, half, 1),
        lax.dynamic_slice_in_dim(exponents, core * half_blocks, half_blocks, 1),
    ).astype(jnp.bfloat16)
    both = jnp.concatenate([scaled, lax.dynamic_slice_in_dim(out_grad, core * half, half, 1)], axis=1)
    sent = contract(pick, both, 1, 0).astype(jnp.bfloat16).reshape(expert_count, 2, width)
    mine = lax.all_to_all(sent, "expert", split_axis=0, concat_axis=0, tiled=True)
    mine = mine.reshape(slot_count, width)
    other = lax.ppermute(mine, "tensor", swap)
    first = jnp.where(core == 0, mine, other)
    second = jnp.where(core == 0, other, mine)
    slot_rows = jnp.concatenate([first[:, :half], second[:, :half]], axis=1)
    slot_grads = jnp.concatenate([first[:, half:], second[:, half:]], axis=1)

    my_slots = lax.dynamic_index_in_dim(slots, my_expert, 0, keepdims=False)
    rank = jnp.sum((my_slots[:, None] > my_slots[None, :]).astype(jnp.int32), axis=1)
    placed = rank[None, :] == jnp.arange(slot_count)[:, None]
    gate_row = jnp.sum(jnp.where(placed, gates, 0.0), axis=1)
    weight_in = w_in[0]
    weight_out = w_out[0]
    preact = jnp.dot(slot_rows, weight_in, preferred_element_type=jnp.float32)
    hidden_full, backward = jax.vjp(jax.nn.gelu, preact)
    hidden = hidden_full.astype(jnp.bfloat16)
    upstream = contract(slot_grads, weight_out, 1, 1)
    gate_part = jnp.sum(hidden.astype(jnp.float32) * upstream, axis=1)
    gate_part = jnp.sum(jnp.where(placed, gate_part[:, None], 0.0), axis=0)
    dpre = backward(gate_row[:, None] * upstream)[0].astype(jnp.bfloat16)
    gated_grads = (gate_row[:, None] * slot_grads.astype(jnp.float32)).astype(jnp.bfloat16)

    keep_weight = lax.dynamic_slice_in_dim(weight_in, core * half, half, 0)
    give_weight = lax.dynamic_slice_in_dim(weight_in, (1 - core) * half, half, 0)
    given = contract(dpre, give_weight, 1, 1).astype(jnp.bfloat16)
    taken = lax.ppermute(given, "tensor", swap)
    chip_back = (contract(dpre, keep_weight, 1, 1) + taken.astype(jnp.float32)).astype(jnp.bfloat16)
    came_back = lax.all_to_all(
        chip_back.reshape(expert_count, 2, half), "expert", split_axis=0, concat_axis=0, tiled=True
    )
    out_weight_grad = contract(hidden, gated_grads, 0, 0).astype(jnp.bfloat16)
    in_weight_grad = contract(slot_rows, dpre, 0, 0).astype(jnp.bfloat16)
    token_sums = contract(pick, came_back.reshape(slot_count, half), 0, 0).astype(jnp.bfloat16)

    share = tok_count // tensor_count
    gate_high = gate_part.astype(jnp.bfloat16)
    gate_low = (gate_part - gate_high.astype(jnp.float32)).astype(jnp.bfloat16)
    gate_rows = jnp.zeros((share, slot_count), jnp.bfloat16).at[0].set(gate_high).at[1].set(gate_low)
    packed = jnp.concatenate(
        [
            token_sums.reshape(tensor_count, share, half),
            jnp.broadcast_to(gate_rows[None], (tensor_count, share, slot_count)),
        ],
        axis=2,
    )
    arrived = lax.all_to_all(packed, "tensor", split_axis=0, concat_axis=0, tiled=True)
    summed = jnp.sum(arrived.astype(jnp.float32).reshape(tensor_count // 2, 2, share, -1), axis=0)
    my_share = jnp.concatenate([summed[0, :, :half], summed[1, :, :half]], axis=1)
    gate_total = jnp.sum(summed[:, :2, half:], axis=(0, 1))
    my_scales = lax.dynamic_slice_in_dim(exponents, my_tensor * share, share, 0)
    token_grad = apply_scales(my_share, my_scales).astype(jnp.bfloat16)
    return (token_grad, in_weight_grad[None], out_weight_grad[None], gate_total[None])


def solution(mesh):
    placed = (
        P("expert", None),
        P("expert", None),
        P("expert", None),
        P(),
        P("expert", None),
        P("expert", None, "tensor"),
        P("expert", "tensor", None),
    )
    return jax.shard_map(
        local,
        mesh=mesh,
        in_specs=placed,
        out_specs=(
            P(("expert", "tensor"), None),
            P("expert", None, "tensor"),
            P("expert", "tensor", None),
            P("expert", None),
        ),
        check_vma=False,
    )
```

```python
import jax
import jax.numpy as jnp
from jax import lax
from jax.experimental import pallas as pl
from jax.experimental.pallas import tpu as pltpu
from jax.sharding import PartitionSpec as P


def contract(left, right, left_dim, right_dim):
    return lax.dot_general(
        left, right, (((left_dim,), (right_dim,)), ((), ())), preferred_element_type=jnp.float32
    )


def apply_scales(values, exponents):
    row_count = values.shape[0]
    block_count = exponents.shape[1]
    factors = jnp.exp2(exponents.astype(jnp.float32))
    widened = values.astype(jnp.float32).reshape(row_count, block_count, 128) * factors[:, :, None]
    return widened.reshape(row_count, block_count * 128)


def place_of(expert, expert_count):
    planes = expert_count // 4
    plane, turned, bit = expert // 4, 0, 1
    while bit < planes:
        turned = turned * 2 + plane // bit % 2
        bit *= 2
    return turned * 4 + expert % 4


SPLIT = 4


def iota(shape, dim):
    return lax.broadcasted_iota(jnp.int32, shape, dim)


def one_hot(hit):
    return hit.astype(jnp.float32).astype(jnp.bfloat16)


def pick_kernel(
    slots_hbm, tokens_hbm, exponents_hbm, grads_hbm, sent_ref, pick_ref, slots, tokens, exponents, grads, done
):
    expert_count, slot_count = slots.shape
    tok_count, part = tokens.shape
    me = lax.axis_index("expert")
    quarter = lax.axis_index("tensor") % SPLIT
    columns = pl.ds(pl.multiple_of(quarter * part, part), part)
    copies = [
        pltpu.make_async_copy(source, target, done.at[index])
        for index, (source, target) in enumerate(
            [
                (slots_hbm, slots),
                (exponents_hbm, exponents),
                (tokens_hbm.at[:, columns], tokens),
                (grads_hbm.at[:, columns], grads),
            ]
        )
    ]
    for copy in copies:
        copy.start()
    row = iota((slot_count, slot_count), 0)
    source = place_of(row // 2, expert_count) + (row % 2) * expert_count
    spread = one_hot(source == iota((slot_count, slot_count), 1))
    token = iota((expert_count, tok_count), 1)
    blocks = exponents.shape[0]
    lanes = iota((blocks, part), 1) // 128 + quarter * (part // 128)
    widen = one_hot(lanes == iota((blocks, part), 0))
    copies[0].wait()
    local_index = slots[...] - me * tok_count
    from_here = (local_index >= 0) & (local_index < tok_count)
    lower = jnp.min(jnp.where(from_here, local_index, tok_count), axis=1, keepdims=True)
    upper = jnp.max(jnp.where(from_here, local_index, -1), axis=1, keepdims=True)
    hits = jnp.concatenate([one_hot(token == lower), one_hot(token == upper)], axis=0)
    pick = contract(spread, hits, 1, 0).astype(jnp.bfloat16)
    pick_ref[...] = pick
    copies[1].wait()
    factors = jnp.exp2(exponents[...].astype(jnp.float32)).astype(jnp.bfloat16)
    scales = contract(factors, widen, 0, 0)
    copies[2].wait()
    scaled = (tokens[...].astype(jnp.float32) * scales).astype(jnp.bfloat16)
    sent_ref[:, :, :part] = contract(pick, scaled, 1, 0).reshape(expert_count, 2, part).astype(jnp.bfloat16)
    copies[3].wait()
    sent_ref[:, :, part:] = contract(pick, grads[...], 1, 0).reshape(expert_count, 2, part).astype(jnp.bfloat16)


def pick_rows(slots, tokens, exponents, out_grad):
    expert_count, slot_count = slots.shape
    tok_count, width = tokens.shape
    part = width // SPLIT
    anywhere = pl.BlockSpec(memory_space=pl.ANY)
    vmem = pl.BlockSpec(memory_space=pltpu.VMEM)
    return pl.pallas_call(
        pick_kernel,
        in_specs=[anywhere] * 4,
        out_specs=[vmem, vmem],
        out_shape=[
            jax.ShapeDtypeStruct((expert_count, 2, 2 * part), jnp.bfloat16),
            pltpu.VMEM((slot_count, tok_count), jnp.bfloat16),
        ],
        scratch_shapes=[
            pltpu.VMEM(slots.shape, jnp.int32),
            pltpu.VMEM((tok_count, part), jnp.bfloat16),
            pltpu.VMEM(exponents.shape[::-1], jnp.int32),
            pltpu.VMEM((tok_count, part), jnp.bfloat16),
            pltpu.SemaphoreType.DMA((4,)),
        ],
        name="pick_rows",
    )(slots, tokens, exponents.T, out_grad)


def hold_kernel(source, target, done):
    copy = pltpu.make_async_copy(source, target, done)
    copy.start()
    copy.wait()


def hold(array):
    return pl.pallas_call(
        hold_kernel,
        in_specs=[pl.BlockSpec(memory_space=pl.ANY)],
        out_specs=pl.BlockSpec(memory_space=pltpu.VMEM),
        out_shape=pltpu.VMEM(array.shape, array.dtype),
        scratch_shapes=[pltpu.SemaphoreType.DMA(())],
        name="hold",
    )(array)


def local(tokens, exponents, out_grad, slots, gates, w_in, w_out):
    expert_count = lax.axis_size("expert")
    tensor_count = lax.axis_size("tensor")
    my_expert = lax.axis_index("expert")
    my_tensor = lax.axis_index("tensor")
    core = my_tensor % 2
    chips = [[index, index + 1] for index in range(0, tensor_count, 2)]
    teams = [list(range(index, index + SPLIT)) for index in range(0, tensor_count, SPLIT)]
    order = [[place_of(index, expert_count) for index in range(expert_count)]]
    tok_count, width = tokens.shape
    half = width // 2
    part = width // SPLIT
    slot_count = slots.shape[1]

    def exchange(rows):
        chunks = rows.reshape(expert_count, 2, rows.shape[1])
        return lax.all_to_all(
            chunks, "expert", split_axis=0, concat_axis=0, axis_index_groups=order, tiled=True
        ).reshape(rows.shape)

    sent, pick = pick_rows(slots, tokens, exponents, out_grad)
    mine = exchange(sent.reshape(slot_count, 2 * part))
    my_slots = lax.dynamic_index_in_dim(slots, my_expert, 0, keepdims=False)
    rank = jnp.sum((my_slots[:, None] > my_slots[None, :]).astype(jnp.int32), axis=1)
    place = place_of(rank // 2, expert_count) * 2 + rank % 2
    placed = place[None, :] == jnp.arange(slot_count)[:, None]
    gate_row = jnp.sum(jnp.where(placed, gates, 0.0), axis=1)
    weight_out = hold(w_out[0])
    mine, gate_row, weight_out = lax.optimization_barrier((mine, gate_row, weight_out))
    joined = lax.all_gather(mine, "tensor", axis_index_groups=teams, axis=0)
    slot_rows = jnp.concatenate([joined[index, :, :part] for index in range(SPLIT)], axis=1)
    slot_grads = jnp.concatenate([joined[index, :, part:] for index in range(SPLIT)], axis=1)

    weight_in = w_in[0]
    preact = jnp.dot(slot_rows, weight_in, preferred_element_type=jnp.float32)
    hidden_full, backward = jax.vjp(jax.nn.gelu, preact)
    hidden = hidden_full.astype(jnp.bfloat16)
    upstream = contract(slot_grads, weight_out, 1, 1)
    gate_part = jnp.sum(hidden.astype(jnp.float32) * upstream, axis=1)
    gate_part = jnp.sum(jnp.where(placed, gate_part[:, None], 0.0), axis=0)
    dpre = backward(gate_row[:, None] * upstream)[0].astype(jnp.bfloat16)
    gated_grads = (gate_row[:, None] * slot_grads.astype(jnp.float32)).astype(jnp.bfloat16)

    keep_weight = lax.dynamic_slice_in_dim(weight_in, core * half, half, 0)
    give_weight = lax.dynamic_slice_in_dim(weight_in, (1 - core) * half, half, 0)
    given = contract(dpre, give_weight, 1, 1).astype(jnp.bfloat16)
    both = lax.all_gather(given, "tensor", axis_index_groups=chips, axis=0)
    taken = lax.dynamic_index_in_dim(both, 1 - core, 0, keepdims=False)
    chip_back = (contract(dpre, keep_weight, 1, 1) + taken.astype(jnp.float32)).astype(jnp.bfloat16)
    came_back = exchange(chip_back)
    out_weight_grad = contract(hidden, gated_grads, 0, 0).astype(jnp.bfloat16)
    in_weight_grad = contract(slot_rows, dpre, 0, 0).astype(jnp.bfloat16)
    token_sums = contract(pick, came_back, 0, 0).astype(jnp.bfloat16)

    share = tok_count // tensor_count
    gate_high = gate_part.astype(jnp.bfloat16)
    gate_low = (gate_part - gate_high.astype(jnp.float32)).astype(jnp.bfloat16)
    gate_rows = jnp.zeros((share, slot_count), jnp.bfloat16).at[0].set(gate_high).at[1].set(gate_low)
    packed = jnp.concatenate(
        [
            token_sums.reshape(tensor_count, share, half),
            jnp.broadcast_to(gate_rows[None], (tensor_count, share, slot_count)),
        ],
        axis=2,
    )
    arrived = lax.all_to_all(packed, "tensor", split_axis=0, concat_axis=0, tiled=True)
    summed = jnp.sum(arrived.astype(jnp.float32).reshape(tensor_count // 2, 2, share, -1), axis=0)
    my_share = jnp.concatenate([summed[0, :, :half], summed[1, :, :half]], axis=1)
    gate_total = jnp.sum(summed[:, :2, half:], axis=(0, 1))
    my_scales = lax.dynamic_slice_in_dim(exponents, my_tensor * share, share, 0)
    token_grad = apply_scales(my_share, my_scales).astype(jnp.bfloat16)
    return (token_grad, in_weight_grad[None], out_weight_grad[None], gate_total[None])


def solution(mesh):
    placed = (
        P("expert", None),
        P("expert", None),
        P("expert", None),
        P(),
        P("expert", None),
        P("expert", None, "tensor"),
        P("expert", "tensor", None),
    )
    return jax.shard_map(
        local,
        mesh=mesh,
        in_specs=placed,
        out_specs=(
            P(("expert", "tensor"), None),
            P("expert", None, "tensor"),
            P("expert", "tensor", None),
            P("expert", None),
        ),
        check_vma=False,
    )
```

```python
import jax
import jax.numpy as jnp
from jax import lax
from jax.experimental import pallas as pl
from jax.experimental.pallas import tpu as pltpu
from jax.sharding import PartitionSpec as P


def contract(left, right, left_dim, right_dim):
    return lax.dot_general(
        left, right, (((left_dim,), (right_dim,)), ((), ())), preferred_element_type=jnp.float32
    )


def place_of(expert, expert_count):
    planes = expert_count // 4
    plane, turned, bit = expert // 4, 0, 1
    while bit < planes:
        turned = turned * 2 + plane // bit % 2
        bit *= 2
    return turned * 4 + expert % 4


SPLIT = 4


def iota(shape, dim):
    return lax.broadcasted_iota(jnp.int32, shape, dim)


def one_hot(hit):
    return hit.astype(jnp.float32).astype(jnp.bfloat16)


def pick_kernel(
    slots_hbm, tokens_hbm, exponents_hbm, grads_hbm, sent_ref, pick_ref, slots, tokens, exponents, grads, done
):
    expert_count, slot_count = slots.shape
    tok_count, part = tokens.shape
    me = lax.axis_index("expert")
    quarter = lax.axis_index("tensor") % SPLIT
    columns = pl.ds(pl.multiple_of(quarter * part, part), part)
    copies = [
        pltpu.make_async_copy(source, target, done.at[index])
        for index, (source, target) in enumerate(
            [
                (slots_hbm, slots),
                (exponents_hbm, exponents),
                (tokens_hbm.at[:, columns], tokens),
                (grads_hbm.at[:, columns], grads),
            ]
        )
    ]
    for copy in copies:
        copy.start()
    row = iota((slot_count, slot_count), 0)
    source = place_of(row // 2, expert_count) + (row % 2) * expert_count
    spread = one_hot(source == iota((slot_count, slot_count), 1))
    token = iota((expert_count, tok_count), 1)
    blocks = exponents.shape[0]
    lanes = iota((blocks, part), 1) // 128 + quarter * (part // 128)
    widen = one_hot(lanes == iota((blocks, part), 0))
    copies[0].wait()
    local_index = slots[...] - me * tok_count
    from_here = (local_index >= 0) & (local_index < tok_count)
    lower = jnp.min(jnp.where(from_here, local_index, tok_count), axis=1, keepdims=True)
    upper = jnp.max(jnp.where(from_here, local_index, -1), axis=1, keepdims=True)
    hits = jnp.concatenate([one_hot(token == lower), one_hot(token == upper)], axis=0)
    pick = contract(spread, hits, 1, 0).astype(jnp.bfloat16)
    pick_ref[...] = pick
    copies[1].wait()
    factors = jnp.exp2(exponents[...].astype(jnp.float32)).astype(jnp.bfloat16)
    scales = contract(factors, widen, 0, 0)
    copies[2].wait()
    scaled = (tokens[...].astype(jnp.float32) * scales).astype(jnp.bfloat16)
    sent_ref[:, :, :part] = contract(pick, scaled, 1, 0).astype(jnp.bfloat16).reshape(expert_count, 2, part)
    copies[3].wait()
    sent_ref[:, :, part:] = contract(pick, grads[...], 1, 0).astype(jnp.bfloat16).reshape(expert_count, 2, part)


def pick_rows(slots, tokens, exponents, out_grad):
    expert_count, slot_count = slots.shape
    tok_count, width = tokens.shape
    part = width // SPLIT
    anywhere = pl.BlockSpec(memory_space=pl.ANY)
    vmem = pl.BlockSpec(memory_space=pltpu.VMEM)
    return pl.pallas_call(
        pick_kernel,
        in_specs=[anywhere] * 4,
        out_specs=[vmem, vmem],
        out_shape=[
            jax.ShapeDtypeStruct((expert_count, 2, 2 * part), jnp.bfloat16),
            pltpu.VMEM((slot_count, tok_count), jnp.bfloat16),
        ],
        scratch_shapes=[
            pltpu.VMEM(slots.shape, jnp.int32),
            pltpu.VMEM((tok_count, part), jnp.bfloat16),
            pltpu.VMEM(exponents.shape[::-1], jnp.int32),
            pltpu.VMEM((tok_count, part), jnp.bfloat16),
            pltpu.SemaphoreType.DMA((4,)),
        ],
        name="pick_rows",
    )(slots, tokens, exponents.T, out_grad)


def hold_kernel(source, target, done):
    copy = pltpu.make_async_copy(source, target, done)
    copy.start()
    copy.wait()


def hold(array):
    return pl.pallas_call(
        hold_kernel,
        in_specs=[pl.BlockSpec(memory_space=pl.ANY)],
        out_specs=pl.BlockSpec(memory_space=pltpu.VMEM),
        out_shape=pltpu.VMEM(array.shape, array.dtype),
        scratch_shapes=[pltpu.SemaphoreType.DMA(())],
        name="hold",
    )(array)


def local(tokens, exponents, out_grad, slots, gates, w_in, w_out):
    expert_count = lax.axis_size("expert")
    tensor_count = lax.axis_size("tensor")
    my_expert = lax.axis_index("expert")
    my_tensor = lax.axis_index("tensor")
    core = my_tensor % 2
    chips = [[index, index + 1] for index in range(0, tensor_count, 2)]
    teams = [list(range(index, index + SPLIT)) for index in range(0, tensor_count, SPLIT)]
    order = [[place_of(index, expert_count) for index in range(expert_count)]]
    tok_count, width = tokens.shape
    half = width // 2
    part = width // SPLIT
    slot_count = slots.shape[1]

    def exchange(rows):
        chunks = rows.reshape(expert_count, 2, rows.shape[1])
        return lax.all_to_all(
            chunks, "expert", split_axis=0, concat_axis=0, axis_index_groups=order, tiled=True
        ).reshape(rows.shape)

    sent, pick = pick_rows(slots, tokens, exponents, out_grad)
    mine = exchange(sent.reshape(slot_count, 2 * part))
    my_slots = lax.dynamic_index_in_dim(slots, my_expert, 0, keepdims=False)
    rank = jnp.sum((my_slots[:, None] > my_slots[None, :]).astype(jnp.int32), axis=1)
    place = place_of(rank // 2, expert_count) * 2 + rank % 2
    placed = place[None, :] == jnp.arange(slot_count)[:, None]
    gate_row = jnp.sum(jnp.where(placed, gates, 0.0), axis=1)
    weight_out = hold(w_out[0])
    mine, gate_row, weight_out = lax.optimization_barrier((mine, gate_row, weight_out))
    joined = lax.all_gather(mine, "tensor", axis_index_groups=teams, axis=0)
    slot_rows = jnp.concatenate([joined[index, :, :part] for index in range(SPLIT)], axis=1)
    slot_grads = jnp.concatenate([joined[index, :, part:] for index in range(SPLIT)], axis=1)

    weight_in = w_in[0]
    preact = jnp.dot(slot_rows, weight_in, preferred_element_type=jnp.float32)
    hidden_full, backward = jax.vjp(jax.nn.gelu, preact)
    hidden = hidden_full.astype(jnp.bfloat16)
    upstream = contract(slot_grads, weight_out, 1, 1)
    gate_part = jnp.sum(hidden.astype(jnp.float32) * upstream, axis=1)
    gate_part = jnp.sum(jnp.where(placed, gate_part[:, None], 0.0), axis=0)
    dpre = backward(gate_row[:, None] * upstream)[0].astype(jnp.bfloat16)
    gated_grads = (gate_row[:, None] * slot_grads.astype(jnp.float32)).astype(jnp.bfloat16)

    keep_weight = lax.dynamic_slice_in_dim(weight_in, core * half, half, 0)
    give_weight = lax.dynamic_slice_in_dim(weight_in, (1 - core) * half, half, 0)
    given = contract(dpre, give_weight, 1, 1).astype(jnp.bfloat16)
    both = lax.all_gather(given, "tensor", axis_index_groups=chips, axis=0)
    taken = lax.dynamic_index_in_dim(both, 1 - core, 0, keepdims=False)
    chip_back = (contract(dpre, keep_weight, 1, 1) + taken.astype(jnp.float32)).astype(jnp.bfloat16)
    came_back = exchange(chip_back)
    out_weight_grad = contract(hidden, gated_grads, 0, 0).astype(jnp.bfloat16)
    in_weight_grad = contract(slot_rows, dpre, 0, 0).astype(jnp.bfloat16)
    came_back, out_weight_grad, in_weight_grad = lax.optimization_barrier(
        (came_back, out_weight_grad, in_weight_grad)
    )
    token_sums = contract(pick, came_back, 0, 0).astype(jnp.bfloat16)

    share = tok_count // tensor_count
    gate_high = gate_part.astype(jnp.bfloat16)
    gate_low = (gate_part - gate_high.astype(jnp.float32)).astype(jnp.bfloat16)
    gate_rows = jnp.zeros((share, slot_count), jnp.bfloat16).at[0].set(gate_high).at[1].set(gate_low)
    packed = jnp.concatenate(
        [
            token_sums.reshape(tensor_count, share, half),
            jnp.broadcast_to(gate_rows[None], (tensor_count, share, slot_count)),
        ],
        axis=2,
    )
    my_exponents = lax.dynamic_slice_in_dim(exponents, my_tensor * share, share, 0)
    scales = jnp.repeat(jnp.exp2(my_exponents.astype(jnp.float32)), 128, axis=1)
    packed, scales = lax.optimization_barrier((packed, scales))
    arrived = lax.all_to_all(packed, "tensor", split_axis=0, concat_axis=0, tiled=True)
    halves = jnp.sum(arrived.astype(jnp.float32).reshape(tensor_count // 2, 2, share, -1), axis=0)
    gate_total = jnp.sum(halves[:, :2, half:], axis=(0, 1))
    my_share = jnp.concatenate([halves[0, :, :half], halves[1, :, :half]], axis=1)
    token_grad = (my_share * scales).astype(jnp.bfloat16)
    return (token_grad, in_weight_grad[None], out_weight_grad[None], gate_total[None])


def solution(mesh):
    placed = (
        P("expert", None),
        P("expert", None),
        P("expert", None),
        P(),
        P("expert", None),
        P("expert", None, "tensor"),
        P("expert", "tensor", None),
    )
    return jax.shard_map(
        local,
        mesh=mesh,
        in_specs=placed,
        out_specs=(
            P(("expert", "tensor"), None),
            P("expert", None, "tensor"),
            P("expert", "tensor", None),
            P("expert", None),
        ),
        check_vma=False,
    )
```

```python
import jax
import jax.numpy as jnp
from jax import lax
from jax.experimental import pallas as pl
from jax.experimental.pallas import tpu as pltpu
from jax.sharding import PartitionSpec as P


def contract(left, right, left_dim, right_dim):
    return lax.dot_general(
        left, right, (((left_dim,), (right_dim,)), ((), ())), preferred_element_type=jnp.float32
    )


def place_of(expert, expert_count):
    planes = expert_count // 4
    plane, turned, bit = expert // 4, 0, 1
    while bit < planes:
        turned = turned * 2 + plane // bit % 2
        bit *= 2
    return turned * 4 + expert % 4


SPLIT = 4


def iota(shape, dim):
    return lax.broadcasted_iota(jnp.int32, shape, dim)


def one_hot(hit):
    return hit.astype(jnp.float32).astype(jnp.bfloat16)


def pick_kernel(
    slots_hbm, tokens_hbm, exponents_hbm, grads_hbm, sent_ref, pick_ref, slots, tokens, exponents, grads, done
):
    expert_count, slot_count = slots.shape
    tok_count, part = tokens.shape
    me = lax.axis_index("expert")
    quarter = lax.axis_index("tensor") % SPLIT
    columns = pl.ds(pl.multiple_of(quarter * part, part), part)
    copies = [
        pltpu.make_async_copy(source, target, done.at[index])
        for index, (source, target) in enumerate(
            [
                (slots_hbm, slots),
                (exponents_hbm, exponents),
                (tokens_hbm.at[:, columns], tokens),
                (grads_hbm.at[:, columns], grads),
            ]
        )
    ]
    for copy in copies:
        copy.start()
    row = iota((slot_count, slot_count), 0)
    source = place_of(row // 2, expert_count) + (row % 2) * expert_count
    spread = one_hot(source == iota((slot_count, slot_count), 1))
    token = iota((expert_count, tok_count), 1)
    blocks = exponents.shape[0]
    lanes = iota((blocks, part), 1) // 128 + quarter * (part // 128)
    widen = one_hot(lanes == iota((blocks, part), 0))
    copies[0].wait()
    local_index = slots[...] - me * tok_count
    from_here = (local_index >= 0) & (local_index < tok_count)
    lower = jnp.min(jnp.where(from_here, local_index, tok_count), axis=1, keepdims=True)
    upper = jnp.max(jnp.where(from_here, local_index, -1), axis=1, keepdims=True)
    hits = jnp.concatenate([one_hot(token == lower), one_hot(token == upper)], axis=0)
    pick = contract(spread, hits, 1, 0).astype(jnp.bfloat16)
    pick_ref[...] = pick
    copies[1].wait()
    factors = jnp.exp2(exponents[...].astype(jnp.float32)).astype(jnp.bfloat16)
    scales = contract(factors, widen, 0, 0)
    copies[2].wait()
    scaled = (tokens[...].astype(jnp.float32) * scales).astype(jnp.bfloat16)
    sent_ref[:, :, :part] = contract(pick, scaled, 1, 0).astype(jnp.bfloat16).reshape(expert_count, 2, part)
    copies[3].wait()
    sent_ref[:, :, part:] = contract(pick, grads[...], 1, 0).astype(jnp.bfloat16).reshape(expert_count, 2, part)


def pick_rows(slots, tokens, exponents, out_grad):
    expert_count, slot_count = slots.shape
    tok_count, width = tokens.shape
    part = width // SPLIT
    anywhere = pl.BlockSpec(memory_space=pl.ANY)
    vmem = pl.BlockSpec(memory_space=pltpu.VMEM)
    return pl.pallas_call(
        pick_kernel,
        in_specs=[anywhere] * 4,
        out_specs=[vmem, vmem],
        out_shape=[
            jax.ShapeDtypeStruct((expert_count, 2, 2 * part), jnp.bfloat16),
            pltpu.VMEM((slot_count, tok_count), jnp.bfloat16),
        ],
        scratch_shapes=[
            pltpu.VMEM(slots.shape, jnp.int32),
            pltpu.VMEM((tok_count, part), jnp.bfloat16),
            pltpu.VMEM(exponents.shape[::-1], jnp.int32),
            pltpu.VMEM((tok_count, part), jnp.bfloat16),
            pltpu.SemaphoreType.DMA((4,)),
        ],
        name="pick_rows",
    )(slots, tokens, exponents.T, out_grad)


def hold_kernel(source, target, done):
    copy = pltpu.make_async_copy(source, target, done)
    copy.start()
    copy.wait()


def hold(array):
    return pl.pallas_call(
        hold_kernel,
        in_specs=[pl.BlockSpec(memory_space=pl.ANY)],
        out_specs=pl.BlockSpec(memory_space=pltpu.VMEM),
        out_shape=pltpu.VMEM(array.shape, array.dtype),
        scratch_shapes=[pltpu.SemaphoreType.DMA(())],
        name="hold",
    )(array)


def in_vmem(*arrays):
    return [pltpu.with_memory_space_constraint(array, pltpu.VMEM) for array in arrays]


def back_kernel(dpre_ref, weight_ref, other_weight_ref, back_ref):
    half = other_weight_ref.shape[1]
    core = lax.axis_index("tensor") % 2
    columns = pl.ds(pl.multiple_of(core * half, half), half)
    total = contract(dpre_ref[core], weight_ref[columns, :], 1, 1)
    total += contract(dpre_ref[1 - core], other_weight_ref[1 - core], 1, 1)
    back_ref[...] = total.astype(jnp.bfloat16).reshape(back_ref.shape)


def chip_sums(dpre, weight_in, other_weights):
    slot_count, half = dpre.shape[1], other_weights.shape[1]
    return pl.pallas_call(
        back_kernel,
        in_specs=[pl.BlockSpec(memory_space=pltpu.VMEM)] * 3,
        out_specs=pl.BlockSpec(memory_space=pltpu.VMEM),
        out_shape=jax.ShapeDtypeStruct((slot_count // 2, 2, half), jnp.bfloat16),
        name="chip_sums",
    )(*in_vmem(dpre, weight_in, other_weights))


def finish_kernel(arrived_ref, scales_ref, token_grad_ref, gate_ref):
    devices = arrived_ref.shape[0]
    half = token_grad_ref.shape[1] // 2
    first = arrived_ref[0].astype(jnp.float32)
    second = arrived_ref[1].astype(jnp.float32)
    for index in range(2, devices, 2):
        first += arrived_ref[index].astype(jnp.float32)
        second += arrived_ref[index + 1].astype(jnp.float32)
    token_grad_ref[:, :half] = (first[:, :half] * scales_ref[:, :half]).astype(jnp.bfloat16)
    token_grad_ref[:, half:] = (second[:, :half] * scales_ref[:, half:]).astype(jnp.bfloat16)
    gates = first[:, half:] + second[:, half:]
    gate_ref[...] = gates[0:1] + gates[1:2]


def finish(arrived, scales, slot_count):
    return pl.pallas_call(
        finish_kernel,
        in_specs=[pl.BlockSpec(memory_space=pltpu.VMEM)] * 2,
        out_specs=[pl.BlockSpec(memory_space=pltpu.VMEM)] * 2,
        out_shape=[
            jax.ShapeDtypeStruct(scales.shape, jnp.bfloat16),
            jax.ShapeDtypeStruct((1, slot_count), jnp.float32),
        ],
        name="finish",
    )(*in_vmem(arrived, scales))


def local(tokens, exponents, out_grad, slots, gates, w_in, w_out):
    expert_count = lax.axis_size("expert")
    tensor_count = lax.axis_size("tensor")
    my_expert = lax.axis_index("expert")
    my_tensor = lax.axis_index("tensor")
    core = my_tensor % 2
    chips = [[index, index + 1] for index in range(0, tensor_count, 2)]
    teams = [list(range(index, index + SPLIT)) for index in range(0, tensor_count, SPLIT)]
    order = [[place_of(index, expert_count) for index in range(expert_count)]]
    tok_count, width = tokens.shape
    half = width // 2
    part = width // SPLIT
    slot_count = slots.shape[1]

    def exchange(chunks):
        return lax.all_to_all(
            chunks, "expert", split_axis=0, concat_axis=0, axis_index_groups=order, tiled=True
        ).reshape(slot_count, chunks.shape[2])

    sent, pick = pick_rows(slots, tokens, exponents, out_grad)
    mine = exchange(sent)
    my_slots = lax.dynamic_index_in_dim(slots, my_expert, 0, keepdims=False)
    rank = jnp.sum((my_slots[:, None] > my_slots[None, :]).astype(jnp.int32), axis=1)
    place = place_of(rank // 2, expert_count) * 2 + rank % 2
    placed = place[None, :] == jnp.arange(slot_count)[:, None]
    gate_row = jnp.sum(jnp.where(placed, gates, 0.0), axis=1)
    weight_out = hold(w_out[0])
    give_weight = lax.dynamic_slice_in_dim(w_in[0], (1 - core) * half, half, 0)
    other_weights = lax.all_gather(give_weight, "tensor", axis_index_groups=chips, axis=0)
    mine, gate_row, weight_out, other_weights = lax.optimization_barrier(
        (mine, gate_row, weight_out, other_weights)
    )
    joined = lax.all_gather(mine, "tensor", axis_index_groups=teams, axis=0)
    slot_rows = jnp.concatenate([joined[index, :, :part] for index in range(SPLIT)], axis=1)
    slot_grads = jnp.concatenate([joined[index, :, part:] for index in range(SPLIT)], axis=1)

    weight_in = w_in[0]
    preact = jnp.dot(slot_rows, weight_in, preferred_element_type=jnp.float32)
    hidden_full, backward = jax.vjp(jax.nn.gelu, preact)
    hidden = hidden_full.astype(jnp.bfloat16)
    upstream = contract(slot_grads, weight_out, 1, 1)
    gate_part = jnp.sum(hidden.astype(jnp.float32) * upstream, axis=1)
    gate_part = jnp.sum(jnp.where(placed, gate_part[:, None], 0.0), axis=0)
    dpre = backward(gate_row[:, None] * upstream)[0].astype(jnp.bfloat16)
    gated_grads = (gate_row[:, None] * slot_grads.astype(jnp.float32)).astype(jnp.bfloat16)

    both = lax.all_gather(dpre, "tensor", axis_index_groups=chips, axis=0)
    chip_back = chip_sums(both, weight_in, other_weights)
    came_back = exchange(chip_back)
    out_weight_grad = contract(hidden, gated_grads, 0, 0).astype(jnp.bfloat16)
    in_weight_grad = contract(slot_rows, dpre, 0, 0).astype(jnp.bfloat16)
    came_back, out_weight_grad, in_weight_grad = lax.optimization_barrier(
        (came_back, out_weight_grad, in_weight_grad)
    )
    token_sums = contract(pick, came_back, 0, 0).astype(jnp.bfloat16)

    share = tok_count // tensor_count
    gate_high = gate_part.astype(jnp.bfloat16)
    gate_low = (gate_part - gate_high.astype(jnp.float32)).astype(jnp.bfloat16)
    gate_rows = jnp.zeros((share, slot_count), jnp.bfloat16).at[0].set(gate_high).at[1].set(gate_low)
    packed = jnp.concatenate(
        [
            token_sums.reshape(tensor_count, share, half),
            jnp.broadcast_to(gate_rows[None], (tensor_count, share, slot_count)),
        ],
        axis=2,
    )
    my_exponents = lax.dynamic_slice_in_dim(exponents, my_tensor * share, share, 0)
    scales = jnp.repeat(jnp.exp2(my_exponents.astype(jnp.float32)), 128, axis=1)
    packed, scales = lax.optimization_barrier((packed, scales))
    arrived = lax.all_to_all(packed, "tensor", split_axis=0, concat_axis=0, tiled=True)
    token_grad, gate_total = finish(arrived, scales, slot_count)
    return (token_grad, in_weight_grad[None], out_weight_grad[None], gate_total)


def solution(mesh):
    placed = (
        P("expert", None),
        P("expert", None),
        P("expert", None),
        P(),
        P("expert", None),
        P("expert", None, "tensor"),
        P("expert", "tensor", None),
    )
    return jax.shard_map(
        local,
        mesh=mesh,
        in_specs=placed,
        out_specs=(
            P(("expert", "tensor"), None),
            P("expert", None, "tensor"),
            P("expert", "tensor", None),
            P("expert", None),
        ),
        check_vma=False,
    )
```

```python
import jax
import jax.numpy as jnp
from jax import lax
from jax.experimental import pallas as pl
from jax.experimental.pallas import tpu as pltpu
from jax.sharding import PartitionSpec as P


def contract(left, right, left_dim, right_dim):
    return lax.dot_general(
        left, right, (((left_dim,), (right_dim,)), ((), ())), preferred_element_type=jnp.float32
    )


def place_of(expert, expert_count):
    planes = expert_count // 4
    plane, turned, bit = expert // 4, 0, 1
    while bit < planes:
        turned = turned * 2 + plane // bit % 2
        bit *= 2
    return turned * 4 + expert % 4


SPLIT = 4


def iota(shape, dim):
    return lax.broadcasted_iota(jnp.int32, shape, dim)


def one_hot(hit):
    return hit.astype(jnp.float32).astype(jnp.bfloat16)


def copy_lanes(source, target, start, count, done):
    lanes = pl.ds(start, count)
    copy = pltpu.make_async_copy(source.at[:, :, lanes], target.at[:, :, lanes], done)
    copy.start()
    return copy


def pick_kernel(
    slots_hbm, tokens_hbm, exponents_hbm, grads_hbm, sent_hbm, pick_ref, slots, tokens, exponents, grads, sent_ref, done
):
    expert_count, slot_count = slots.shape
    tok_count, part = tokens.shape
    me = lax.axis_index("expert")
    quarter = lax.axis_index("tensor") % SPLIT
    columns = pl.ds(pl.multiple_of(quarter * part, part), part)
    copies = [
        pltpu.make_async_copy(source, target, done.at[index])
        for index, (source, target) in enumerate(
            [
                (slots_hbm, slots),
                (exponents_hbm, exponents),
                (tokens_hbm.at[:, columns], tokens),
                (grads_hbm.at[:, columns], grads),
            ]
        )
    ]
    for copy in copies:
        copy.start()
    row = iota((slot_count, slot_count), 0)
    source = place_of(row // 2, expert_count) + (row % 2) * expert_count
    spread = one_hot(source == iota((slot_count, slot_count), 1))
    token = iota((expert_count, tok_count), 1)
    blocks = exponents.shape[0]
    lanes = iota((blocks, part), 1) // 128 + quarter * (part // 128)
    widen = one_hot(lanes == iota((blocks, part), 0))
    copies[0].wait()
    local_index = slots[...] - me * tok_count
    from_here = (local_index >= 0) & (local_index < tok_count)
    lower = jnp.min(jnp.where(from_here, local_index, tok_count), axis=1, keepdims=True)
    upper = jnp.max(jnp.where(from_here, local_index, -1), axis=1, keepdims=True)
    hits = jnp.concatenate([one_hot(token == lower), one_hot(token == upper)], axis=0)
    pick = contract(spread, hits, 1, 0).astype(jnp.bfloat16)
    pick_ref[...] = pick
    copies[1].wait()
    factors = jnp.exp2(exponents[...].astype(jnp.float32)).astype(jnp.bfloat16)
    scales = contract(factors, widen, 0, 0)
    copies[2].wait()
    scaled = (tokens[...].astype(jnp.float32) * scales).astype(jnp.bfloat16)
    sent_ref[:, :, :part] = contract(pick, scaled, 1, 0).astype(jnp.bfloat16).reshape(expert_count, 2, part)
    rows_out = copy_lanes(sent_ref, sent_hbm, 0, part, done.at[4])
    copies[3].wait()
    sent_ref[:, :, part:] = contract(pick, grads[...], 1, 0).astype(jnp.bfloat16).reshape(expert_count, 2, part)
    grads_out = copy_lanes(sent_ref, sent_hbm, part, part, done.at[5])
    rows_out.wait()
    grads_out.wait()


def pick_rows(slots, tokens, exponents, out_grad):
    expert_count, slot_count = slots.shape
    tok_count, width = tokens.shape
    part = width // SPLIT
    anywhere = pl.BlockSpec(memory_space=pl.ANY)
    vmem = pl.BlockSpec(memory_space=pltpu.VMEM)
    return pl.pallas_call(
        pick_kernel,
        in_specs=[anywhere] * 4,
        out_specs=[anywhere, vmem],
        out_shape=[
            jax.ShapeDtypeStruct((expert_count, 2, 2 * part), jnp.bfloat16),
            pltpu.VMEM((slot_count, tok_count), jnp.bfloat16),
        ],
        scratch_shapes=[
            pltpu.VMEM(slots.shape, jnp.int32),
            pltpu.VMEM((tok_count, part), jnp.bfloat16),
            pltpu.VMEM(exponents.shape[::-1], jnp.int32),
            pltpu.VMEM((tok_count, part), jnp.bfloat16),
            pltpu.VMEM((expert_count, 2, 2 * part), jnp.bfloat16),
            pltpu.SemaphoreType.DMA((6,)),
        ],
        name="pick_rows",
    )(slots, tokens, exponents.T, out_grad)


def hold_kernel(source, target, done):
    copy = pltpu.make_async_copy(source, target, done)
    copy.start()
    copy.wait()


def hold(array):
    return pl.pallas_call(
        hold_kernel,
        in_specs=[pl.BlockSpec(memory_space=pl.ANY)],
        out_specs=pl.BlockSpec(memory_space=pltpu.VMEM),
        out_shape=pltpu.VMEM(array.shape, array.dtype),
        scratch_shapes=[pltpu.SemaphoreType.DMA(())],
        name="hold",
    )(array)


def in_vmem(*arrays):
    return [pltpu.with_memory_space_constraint(array, pltpu.VMEM) for array in arrays]


def back_kernel(dpre_ref, weight_ref, other_weight_ref, back_hbm, back_ref, done):
    half = other_weight_ref.shape[1]
    piece = half // 2
    core = lax.axis_index("tensor") % 2
    copies = []
    for index in range(2):
        start = index * piece
        columns = pl.ds(pl.multiple_of(core * half + start, piece), piece)
        total = contract(dpre_ref[core], weight_ref[columns, :], 1, 1)
        total += contract(dpre_ref[1 - core], other_weight_ref[1 - core, start : start + piece, :], 1, 1)
        rows = total.astype(jnp.bfloat16).reshape(back_ref.shape[0], 2, piece)
        back_ref[:, :, start : start + piece] = rows
        copies.append(copy_lanes(back_ref, back_hbm, start, piece, done.at[index]))
    for copy in copies:
        copy.wait()


def chip_sums(dpre, weight_in, other_weights):
    slot_count, half = dpre.shape[1], other_weights.shape[1]
    return pl.pallas_call(
        back_kernel,
        in_specs=[pl.BlockSpec(memory_space=pltpu.VMEM)] * 3,
        out_specs=pl.BlockSpec(memory_space=pl.ANY),
        out_shape=jax.ShapeDtypeStruct((slot_count // 2, 2, half), jnp.bfloat16),
        scratch_shapes=[
            pltpu.VMEM((slot_count // 2, 2, half), jnp.bfloat16),
            pltpu.SemaphoreType.DMA((2,)),
        ],
        name="chip_sums",
    )(*in_vmem(dpre, weight_in, other_weights))


def finish_kernel(arrived_ref, scales_ref, token_grad_ref, gate_ref):
    devices = arrived_ref.shape[0]
    half = token_grad_ref.shape[1] // 2
    first = arrived_ref[0].astype(jnp.float32)
    second = arrived_ref[1].astype(jnp.float32)
    for index in range(2, devices, 2):
        first += arrived_ref[index].astype(jnp.float32)
        second += arrived_ref[index + 1].astype(jnp.float32)
    token_grad_ref[:, :half] = (first[:, :half] * scales_ref[:, :half]).astype(jnp.bfloat16)
    token_grad_ref[:, half:] = (second[:, :half] * scales_ref[:, half:]).astype(jnp.bfloat16)
    gates = first[:, half:] + second[:, half:]
    gate_ref[...] = gates[0:1] + gates[1:2]


def finish(arrived, scales, slot_count):
    return pl.pallas_call(
        finish_kernel,
        in_specs=[pl.BlockSpec(memory_space=pltpu.VMEM)] * 2,
        out_specs=[pl.BlockSpec(memory_space=pltpu.VMEM)] * 2,
        out_shape=[
            jax.ShapeDtypeStruct(scales.shape, jnp.bfloat16),
            jax.ShapeDtypeStruct((1, slot_count), jnp.float32),
        ],
        name="finish",
    )(*in_vmem(arrived, scales))


def local(tokens, exponents, out_grad, slots, gates, w_in, w_out):
    expert_count = lax.axis_size("expert")
    tensor_count = lax.axis_size("tensor")
    my_expert = lax.axis_index("expert")
    my_tensor = lax.axis_index("tensor")
    core = my_tensor % 2
    chips = [[index, index + 1] for index in range(0, tensor_count, 2)]
    teams = [list(range(index, index + SPLIT)) for index in range(0, tensor_count, SPLIT)]
    order = [[place_of(index, expert_count) for index in range(expert_count)]]
    tok_count, width = tokens.shape
    half = width // 2
    part = width // SPLIT
    slot_count = slots.shape[1]

    def exchange(chunks):
        return lax.all_to_all(
            chunks, "expert", split_axis=0, concat_axis=0, axis_index_groups=order, tiled=True
        ).reshape(slot_count, chunks.shape[2])

    sent, pick = pick_rows(slots, tokens, exponents, out_grad)
    mine = exchange(sent)
    my_slots = lax.dynamic_index_in_dim(slots, my_expert, 0, keepdims=False)
    rank = jnp.sum((my_slots[:, None] > my_slots[None, :]).astype(jnp.int32), axis=1)
    place = place_of(rank // 2, expert_count) * 2 + rank % 2
    placed = place[None, :] == jnp.arange(slot_count)[:, None]
    gate_row = jnp.sum(jnp.where(placed, gates, 0.0), axis=1)
    weight_out = hold(w_out[0])
    give_weight = lax.dynamic_slice_in_dim(w_in[0], (1 - core) * half, half, 0)
    other_weights = lax.all_gather(give_weight, "tensor", axis_index_groups=chips, axis=0)
    mine, gate_row, weight_out, other_weights = lax.optimization_barrier(
        (mine, gate_row, weight_out, other_weights)
    )
    joined = lax.all_gather(mine, "tensor", axis_index_groups=teams, axis=0)
    slot_rows = jnp.concatenate([joined[index, :, :part] for index in range(SPLIT)], axis=1)
    slot_grads = jnp.concatenate([joined[index, :, part:] for index in range(SPLIT)], axis=1)

    weight_in = w_in[0]
    preact = jnp.dot(slot_rows, weight_in, preferred_element_type=jnp.float32)
    hidden_full, backward = jax.vjp(jax.nn.gelu, preact)
    hidden = hidden_full.astype(jnp.bfloat16)
    upstream = contract(slot_grads, weight_out, 1, 1)
    gate_part = jnp.sum(hidden.astype(jnp.float32) * upstream, axis=1)
    gate_part = jnp.sum(jnp.where(placed, gate_part[:, None], 0.0), axis=0)
    dpre = backward(gate_row[:, None] * upstream)[0].astype(jnp.bfloat16)
    gated_grads = (gate_row[:, None] * slot_grads.astype(jnp.float32)).astype(jnp.bfloat16)

    both = lax.all_gather(dpre, "tensor", axis_index_groups=chips, axis=0)
    chip_back = chip_sums(both, weight_in, other_weights)
    came_back = exchange(chip_back)
    out_weight_grad = contract(hidden, gated_grads, 0, 0).astype(jnp.bfloat16)
    in_weight_grad = contract(slot_rows, dpre, 0, 0).astype(jnp.bfloat16)
    came_back, out_weight_grad, in_weight_grad = lax.optimization_barrier(
        (came_back, out_weight_grad, in_weight_grad)
    )
    token_sums = contract(pick, came_back, 0, 0).astype(jnp.bfloat16)

    share = tok_count // tensor_count
    gate_high = gate_part.astype(jnp.bfloat16)
    gate_low = (gate_part - gate_high.astype(jnp.float32)).astype(jnp.bfloat16)
    gate_rows = jnp.zeros((share, slot_count), jnp.bfloat16).at[0].set(gate_high).at[1].set(gate_low)
    packed = jnp.concatenate(
        [
            token_sums.reshape(tensor_count, share, half),
            jnp.broadcast_to(gate_rows[None], (tensor_count, share, slot_count)),
        ],
        axis=2,
    )
    my_exponents = lax.dynamic_slice_in_dim(exponents, my_tensor * share, share, 0)
    scales = jnp.repeat(jnp.exp2(my_exponents.astype(jnp.float32)), 128, axis=1)
    packed, scales = lax.optimization_barrier((packed, scales))
    arrived = lax.all_to_all(packed, "tensor", split_axis=0, concat_axis=0, tiled=True)
    token_grad, gate_total = finish(arrived, scales, slot_count)
    return (token_grad, in_weight_grad[None], out_weight_grad[None], gate_total)


def solution(mesh):
    placed = (
        P("expert", None),
        P("expert", None),
        P("expert", None),
        P(),
        P("expert", None),
        P("expert", None, "tensor"),
        P("expert", "tensor", None),
    )
    return jax.shard_map(
        local,
        mesh=mesh,
        in_specs=placed,
        out_specs=(
            P(("expert", "tensor"), None),
            P("expert", None, "tensor"),
            P("expert", "tensor", None),
            P("expert", None),
        ),
        check_vma=False,
    )
```
